32 devices in a mesh: grp: 8 (over z, y), band: 4 (over x, core).
Axes of the slice: x: 2, y: 2, z: 4, core: 2. Of those that a mesh axis runs over, the one named last changes fastest.
Arguments:
- spectra: bfloat16 [2, 32, 32, 1024], P(None, None, 'band', 'grp'), may hold values from -140 to 140, as said below
- tile_band: int32 [8, 8], P('grp'), may hold values from 0 to 4, as said below
Outputs:
- gathers: bfloat16 [8, 4, 32, 128, 256], P('grp', 'band')
The draws below stay inside these ranges and needn't reach their ends.
Inputs may be any that keep to these rules, and one draw needn't show every extreme that they name: `spectra`: entries are of order one times a scale of each window and channel. `tile_band`: entry (i, j) is |i - j| * 4 // 8, or 4 where the pair is not stacked; it is 4 where i = j, and never 4 where |i - j| = 1.
All inputs are finite; a program needn't handle non-finite values.
Results may differ from the reference program's by a relative error of at most 0.0064.
Values may be sent and summed in bfloat16 or wider, within the bound.
A program may use at most 64 MiB of HBM per device.

```python
import jax
import jax.numpy as jnp
from jax import lax

TILE = 128
WINDOWS = 32
BLOCKS = 8
BANDS = 4
BINS = 32
CHANNELS = 1024


def draw_spectra(key, part):
    entry_key = jax.random.fold_in(key, 11)
    scale_key = jax.random.fold_in(key, 23)
    shape = (2, WINDOWS, BINS, CHANNELS)
    entries = jnp.clip(jax.random.normal(entry_key, shape, jnp.float32), -5.0, 5.0)
    levels = jax.random.uniform(scale_key, (WINDOWS, CHANNELS), jnp.float32, 0.0, jnp.log(10.0))
    rising = jnp.sqrt(3.0 ** (jnp.arange(BINS, dtype=jnp.float32) / max(BINS - 1, 1)))
    return (entries * jnp.exp(levels)[None, :, None, :] * rising[None, None, :, None]).astype(jnp.bfloat16)


def draw_tile_band(key, part):
    rows = jnp.arange(BLOCKS, dtype=jnp.int32)[:, None]
    cols = jnp.arange(BLOCKS, dtype=jnp.int32)[None, :]
    offset = jnp.abs(rows - cols)
    banded = offset * BANDS // BLOCKS
    dropped = (jax.random.randint(jax.random.fold_in(key, 5), (BLOCKS, BLOCKS), 0, 4) == 0) & (offset >= 2)
    return jnp.where((offset == 0) | dropped, BANDS, banded).astype(jnp.int32)


def setup_inputs(seed: int = 0) -> dict:
    key_of = jax.random.split(jax.random.key(seed), 3)
    spectra = draw_spectra(jax.random.fold_in(key_of[2], 71), 0)
    tile_band = draw_tile_band(jax.random.fold_in(key_of[2], 71), 0)
    return dict(spectra=spectra, tile_band=tile_band)


def reference(spectra, tile_band):
    values = spectra.astype(jnp.float32)
    power = lax.optimization_barrier(jnp.sum(values * values, axis=(0, 2)))
    white = (values * lax.rsqrt(power / BINS + 1e-05)[None, :, None, :]).astype(jnp.bfloat16)
    selector = (tile_band[:, None, :] == jnp.arange(BANDS, dtype=jnp.int32)[None, :, None]).astype(jnp.float32)
    counts = lax.optimization_barrier(jnp.sum(selector, axis=2))
    blocks_view = white.astype(jnp.float32).reshape(2, WINDOWS, BINS, BLOCKS, TILE)
    own_all = jnp.moveaxis(blocks_view, 3, 0)

    def one_source(inputs):
        row, weights, own = inputs
        partner = jnp.einsum('kn,pwfnc->kpwfc', row, blocks_view, precision=lax.Precision.HIGHEST)
        partner = lax.optimization_barrier(partner.astype(jnp.bfloat16)).astype(jnp.float32)
        real_part = partner[:, 0]
        imag_part = partner[:, 1]
        paired = jnp.stack([jnp.stack([real_part, imag_part], axis=3), jnp.stack([imag_part, -real_part], axis=3)], axis=1)
        gram = jnp.einsum('pwfa,kpwfqb->kfaqb', own, paired, precision=lax.Precision.HIGHEST)
        gram = gram.reshape(BANDS, BINS, TILE, 2 * TILE)
        return (gram / jnp.maximum(weights, 1.0)[:, None, None, None]).astype(jnp.bfloat16)
    return lax.map(one_source, (selector, counts, own_all))
```

```python
import functools

import jax
import jax.numpy as jnp
from jax import lax
from jax.experimental import pallas as pl
from jax.experimental.pallas import tpu as pltpu
from jax.sharding import PartitionSpec as P

LINES = 4
CHUNKS = 4
MESH = pl.DeviceIdType.MESH


def kernel(
    groups, bands, bins, windows, chunks,
    tb_ref, x_ref, out_ref,
    raw, power, blocks, sums, own, partner,
    p_send, p_recv, line_send, side_send, block_recv, own_send, own_recv, sum_send, sum_recv,
):
    g = lax.axis_index("grp")
    b = lax.axis_index("band")
    inner = groups // LINES
    row, col = g // inner, lax.rem(g, inner)
    rows = 2 * windows
    part = bins // chunks
    half = row // 2
    near = [row + 1 - 2 * lax.rem(row, 2), 2 - half, 3 - 3 * half]
    line = [r * inner + col for r in near]
    side = [lax.rem(col + e, inner) for e in range(1, inner)]
    peer = [lax.rem(b + e, bands) for e in range(bands)]

    barrier = pltpu.get_barrier_semaphore()
    for j in line:
        pl.semaphore_signal(barrier, inc=1, device_id=(j, b), device_id_type=MESH)
    for s in side:
        pl.semaphore_signal(barrier, inc=1, device_id=(row * inner + s, b), device_id_type=MESH)
    for k in peer[1:]:
        pl.semaphore_signal(barrier, inc=1, device_id=(g, k), device_id_type=MESH)

    raw[...] = x_ref[...].astype(jnp.float32)
    total = jnp.zeros((rows, raw.shape[1]), jnp.float32)
    for f in range(bins):
        v = raw[pl.ds(f, rows, stride=bins), :]
        total = total + v * v
    power[b] = total[:windows] + total[windows:]

    pl.semaphore_wait(barrier, len(line) + len(side) + bands - 1)

    def power_copy(e):
        return pltpu.make_async_remote_copy(
            src_ref=power.at[b], dst_ref=power.at[b], send_sem=p_send.at[e - 1], recv_sem=p_recv.at[e - 1],
            device_id=(g, peer[e]), device_id_type=MESH,
        )

    def block_copy(j, c, send_sem, target):
        view = blocks.at[j, pl.ds(c * part, part)]
        return pltpu.make_async_remote_copy(
            src_ref=view, dst_ref=view, send_sem=send_sem, recv_sem=block_recv.at[j, c],
            device_id=(target, b), device_id_type=MESH,
        )

    def line_copy(t, c):
        return block_copy(g, c, line_send.at[t, c], line[t])

    def side_copy(e, r, slot, c):
        return block_copy(r * inner + col, c, side_send.at[e, slot, c], row * inner + side[e])

    def block_wait(j, c):
        block_copy(j, c, line_send.at[0, c], line[0]).wait_recv()

    def own_copy(e):
        return pltpu.make_async_remote_copy(
            src_ref=blocks.at[g], dst_ref=own.at[b], send_sem=own_send.at[e - 1], recv_sem=own_recv.at[e - 1],
            device_id=(g, peer[e]), device_id_type=MESH,
        )

    def sum_copy(e, c):
        return pltpu.make_async_remote_copy(
            src_ref=sums.at[e - 1, pl.ds(c * part, part)], dst_ref=partner.at[b, pl.ds(c * part, part)],
            send_sem=sum_send.at[e - 1, c], recv_sem=sum_recv.at[e - 1, c],
            device_id=(g, peer[e]), device_id_type=MESH,
        )

    for e in range(1, bands):
        power_copy(e).start()
    for e in range(1, bands):
        power_copy(e).wait_recv()
    whole = power[0]
    for e in range(1, bands):
        whole = whole + power[e]
    factor = lax.rsqrt(whole / (bins * bands) + 1e-05)
    factor = jnp.concatenate([factor, factor], axis=0)
    for c in range(chunks):
        for f in range(c * part, (c + 1) * part):
            v = (raw[pl.ds(f, rows, stride=bins), :] * factor).astype(jnp.bfloat16)
            blocks[g, f] = v
            own[b, f] = v
        for e in range(len(side)):
            side_copy(e, row, 0, c).start()
        for t in range(len(line)):
            line_copy(t, c).start()
    for e in range(1, bands):
        own_copy(e).start()

    def forward(c):
        for t in range(len(line)):
            block_wait(line[t], c)
            for e in range(len(side)):
                side_copy(e, near[t], t + 1, c).start()

    def pick(j, k):
        inside = (j >= 0) & (j < groups)
        at = jnp.clip(j, 0, groups - 1)
        return at, jnp.where(inside & (tb_ref[0, at] == k), 1.0, 0.0)

    reach = groups // bands

    def band_sum(c):
        for s in side:
            for r in [row] + near:
                block_wait(r * inner + s, c)
        for e in list(range(1, bands)) + [0]:
            k = peer[e]
            terms = []
            for q in range(reach):
                d = k * reach + q
                terms.append(pick(g + d, k))
                at, weight = pick(g - d, k)
                terms.append((at, jnp.where(d > 0, weight, 0.0)))
            for f in range(c * part, (c + 1) * part):
                acc = None
                for at, weight in terms:
                    term = blocks[at, f].astype(jnp.float32) * weight
                    acc = term if acc is None else acc + term
                acc = acc.astype(jnp.bfloat16)
                if e == 0:
                    partner[b, f] = acc
                else:
                    sums[e - 1, f] = acc
            if e > 0:
                sum_copy(e, c).start()

    count = jnp.float32(0.0)
    for j in range(groups):
        count = count + jnp.where(tb_ref[0, j] == b, 1.0, 0.0)
    scale = 1.0 / jnp.maximum(jnp.full((1, 2 * raw.shape[1]), count, jnp.float32), 1.0)

    def gram(c):
        for e in range(bands):
            if e > 0:
                if c == 0:
                    own_copy(e).wait_recv()
                sum_copy(e, c).wait_recv()
            owner = lax.rem(b + bands - e, bands)
            for f in range(c * part, (c + 1) * part):
                y = partner[owner, f]
                turned = jnp.concatenate([y[windows:], -y[:windows]], axis=0)
                both = jnp.concatenate([y, turned], axis=1)
                tile = lax.dot_general(
                    own[owner, f], both, (((0,), (0,)), ((), ())), preferred_element_type=jnp.float32
                )
                out_ref[owner * bins + f] = (tile * scale).astype(jnp.bfloat16)

    forward(0)
    for c in range(chunks):
        if c + 1 < chunks:
            forward(c + 1)
        band_sum(c)
        if c > 0:
            gram(c - 1)
    gram(chunks - 1)

    for e in range(1, bands):
        power_copy(e).wait_send()
        own_copy(e).wait_send()
    for c in range(chunks):
        for t in range(len(line)):
            line_copy(t, c).wait_send()
        for e in range(len(side)):
            for slot, r in enumerate([row] + near):
                side_copy(e, r, slot, c).wait_send()
        for e in range(1, bands):
            sum_copy(e, c).wait_send()


def local(groups, bands, spectra, tile_band):
    _, windows, bins, tile = spectra.shape
    rows = 2 * windows
    flat = spectra.reshape(rows * bins, tile)
    inner = groups // LINES
    dma = pltpu.SemaphoreType.DMA
    out = pl.pallas_call(
        functools.partial(kernel, groups, bands, bins, windows, CHUNKS),
        out_shape=jax.ShapeDtypeStruct((bands * bins, tile, 2 * tile), jnp.bfloat16),
        in_specs=[pl.BlockSpec(memory_space=pltpu.SMEM), pl.BlockSpec(memory_space=pltpu.VMEM)],
        out_specs=pl.BlockSpec(memory_space=pltpu.VMEM),
        scratch_shapes=[
            pltpu.VMEM((rows * bins, tile), jnp.float32),
            pltpu.VMEM((bands, windows, tile), jnp.float32),
            pltpu.VMEM((groups, bins, rows, tile), jnp.bfloat16),
            pltpu.VMEM((bands - 1, bins, rows, tile), jnp.bfloat16),
            pltpu.VMEM((bands, bins, rows, tile), jnp.bfloat16),
            pltpu.VMEM((bands, bins, rows, tile), jnp.bfloat16),
            dma((bands - 1,)),
            dma((bands - 1,)),
            dma((LINES - 1, CHUNKS)),
            dma((inner - 1, LINES, CHUNKS)),
            dma((groups, CHUNKS)),
            dma((bands - 1,)),
            dma((bands - 1,)),
            dma((bands - 1, CHUNKS)),
            dma((bands - 1, CHUNKS)),
        ],
        compiler_params=pltpu.CompilerParams(
            collective_id=0, has_side_effects=True, vmem_limit_bytes=32 * 1024 * 1024
        ),
    )(tile_band, flat)
    return out.reshape(1, 1, bands * bins, tile, 2 * tile)


def solution(mesh):
    return jax.shard_map(
        functools.partial(local, mesh.shape["grp"], mesh.shape["band"]),
        mesh=mesh,
        in_specs=(P(None, None, "band", "grp"), P("grp", None)),
        out_specs=P("grp", "band", None, None, None),
        check_vma=False,
    )
```

```python
import functools

import jax
import jax.numpy as jnp
from jax import lax
from jax.experimental import pallas as pl
from jax.experimental.pallas import tpu as pltpu
from jax.sharding import PartitionSpec as P

LINES = 4
SHARES = (1, 1, 1, 1)
CHUNKS = len(SHARES)
MESH = pl.DeviceIdType.MESH


def kernel(
    groups, bands, bins, windows, chunks,
    tb_hbm, x_hbm, out_ref,
    tb_ref, x_ref, raw, power, line_raw, side_raw, line_factor, side_factor, blocks, sums, own, partner,
    in_sem, p_send, p_recv, line_send, line_recv, first_send, first_recv, side_send, block_recv,
    lf_send, lf_recv, sf_send, sf_recv, own_send, own_recv, sum_send, sum_recv,
):
    g = lax.axis_index("grp")
    b = lax.axis_index("band")
    inner = groups // LINES
    row, col = g // inner, lax.rem(g, inner)
    rows = 2 * windows
    unit = bins // sum(SHARES)
    sizes = [n * unit for n in SHARES]
    starts = [sum(sizes[:c]) for c in range(chunks)]
    half = row // 2
    others = [row + 1 - 2 * lax.rem(row, 2), 2 - half, 3 - 3 * half]
    side = [lax.rem(col + e, inner) for e in range(1, inner)]
    source = [lax.rem(col + inner - e, inner) for e in range(1, inner)]
    peer = [lax.rem(b + e, bands) for e in range(bands)]

    barrier = pltpu.get_barrier_semaphore()
    for r in others:
        pl.semaphore_signal(barrier, inc=1, device_id=(r * inner + col, b), device_id_type=MESH)
    for s in side:
        pl.semaphore_signal(barrier, inc=1, device_id=(row * inner + s, b), device_id_type=MESH)
    for k in peer[1:]:
        pl.semaphore_signal(barrier, inc=1, device_id=(g, k), device_id_type=MESH)

    load_x = pltpu.make_async_copy(x_hbm, x_ref, in_sem.at[0])
    load_tb = pltpu.make_async_copy(tb_hbm, tb_ref, in_sem.at[1])
    load_x.start()
    load_tb.start()
    load_x.wait()
    raw[...] = x_ref[...].astype(jnp.float32)
    total = jnp.zeros((rows, raw.shape[1]), jnp.float32)
    for f in range(bins):
        v = raw[pl.ds(f, rows, stride=bins), :]
        line_raw[row, f] = v.astype(jnp.bfloat16)
        total = total + v * v
    power[b] = total[:windows] + total[windows:]
    load_tb.wait()

    pl.semaphore_wait(barrier, len(others) + len(side) + bands - 1)

    def remote(src, dst, send_sem, recv_sem, target):
        return pltpu.make_async_remote_copy(
            src_ref=src, dst_ref=dst, send_sem=send_sem, recv_sem=recv_sem,
            device_id=target, device_id_type=MESH,
        )

    def power_copy(e):
        return remote(power.at[b], power.at[b], p_send.at[e - 1], p_recv.at[e - 1], (g, peer[e]))

    def line_copy(r, c, send_sem, to):
        view = line_raw.at[r, pl.ds(starts[c], sizes[c])]
        return remote(view, view, send_sem, line_recv.at[r, c], (to * inner + col, b))

    def own_line_copy(t, c):
        return line_copy(row, c, line_send.at[t, c], others[t])

    def first_copy(e, c):
        return remote(
            line_raw.at[row, pl.ds(starts[c], sizes[c])], side_raw.at[e, pl.ds(starts[c], sizes[c])],
            first_send.at[e, c], first_recv.at[e, c], (row * inner + side[e], b),
        )

    def side_copy(e, r, c):
        j = r * inner + col
        view = blocks.at[j, pl.ds(starts[c], sizes[c])]
        return remote(view, view, side_send.at[e, r, c], block_recv.at[j, c], (row * inner + side[e], b))

    def block_wait(j, c):
        view = blocks.at[j, pl.ds(starts[c], sizes[c])]
        remote(view, view, side_send.at[0, 0, c], block_recv.at[j, c], (g, peer[1])).wait_recv()

    def line_factor_copy(t):
        view = line_factor.at[row]
        return remote(view, view, lf_send.at[t], lf_recv.at[row], (others[t] * inner + col, b))

    def side_factor_copy(e):
        return remote(
            line_factor.at[row], side_factor.at[e], sf_send.at[e], sf_recv.at[e], (row * inner + side[e], b)
        )

    def own_copy(e):
        return remote(blocks.at[g], own.at[b], own_send.at[e - 1], own_recv.at[e - 1], (g, peer[e]))

    def sum_copy(e, c):
        span = pl.ds(starts[c], sizes[c])
        return remote(
            sums.at[e - 1, span], partner.at[b, span], sum_send.at[e - 1, c], sum_recv.at[e - 1, c], (g, peer[e])
        )

    def whiten(value, factor):
        both = jnp.concatenate([factor, factor], axis=0)
        return (value.astype(jnp.float32) * both).astype(jnp.bfloat16)

    for e in range(1, bands):
        power_copy(e).start()
    for c in range(chunks):
        for e in range(len(side)):
            first_copy(e, c).start()
        if c == 0:
            for t in range(len(others)):
                own_line_copy(t, c).start()

    for e in range(1, bands):
        power_copy(e).wait_recv()
    whole = power[0]
    for e in range(1, bands):
        whole = whole + power[e]
    factor = lax.rsqrt(whole / (bins * bands) + 1e-05)
    line_factor[row] = factor
    for t in range(len(others)):
        line_factor_copy(t).start()
    for e in range(len(side)):
        side_factor_copy(e).start()
    for c in range(1, chunks):
        for t in range(len(others)):
            own_line_copy(t, c).start()
    for f in range(bins):
        v = whiten(line_raw[row, f], factor)
        blocks[g, f] = v
        own[b, f] = v
    for e in range(1, bands):
        own_copy(e).start()
    def arrive(r, c):
        j = r * inner + col
        for f in range(starts[c], starts[c] + sizes[c]):
            blocks[j, f] = whiten(line_raw[r, f], line_factor[r])
        for e in range(len(side)):
            side_copy(e, r, c).start()

    def forward(c):
        for r in others:
            if c == 0:
                view = line_factor.at[r]
                remote(view, view, lf_send.at[0], lf_recv.at[r], (g, peer[1])).wait_recv()
            line_copy(r, c, line_send.at[0, c], others[0]).wait_recv()
            arrive(r, c)

    def pick(j, k):
        inside = (j >= 0) & (j < groups)
        at = jnp.clip(j, 0, groups - 1)
        return at, jnp.where(inside & (tb_ref[0, at] == k), 1.0, 0.0)

    reach = groups // bands

    def band_sum(c):
        for e in range(len(side)):
            if c == 0:
                side_factor_copy(e).wait_recv()
            first_copy(e, c).wait_recv()
            for f in range(starts[c], starts[c] + sizes[c]):
                blocks[row * inner + source[e], f] = whiten(side_raw[e, f], side_factor[e])
            for r in others:
                block_wait(r * inner + source[e], c)
        for e in list(range(1, bands)) + [0]:
            k = peer[e]
            terms = []
            for q in range(reach):
                d = k * reach + q
                terms.append(pick(g + d, k))
                at, weight = pick(g - d, k)
                terms.append((at, jnp.where(d > 0, weight, 0.0)))
            for f in range(starts[c], starts[c] + sizes[c]):
                acc = None
                for at, weight in terms:
                    term = blocks[at, f].astype(jnp.float32) * weight
                    acc = term if acc is None else acc + term
                acc = acc.astype(jnp.bfloat16)
                if e == 0:
                    partner[b, f] = acc
                else:
                    sums[e - 1, f] = acc
            if e > 0:
                sum_copy(e, c).start()

    count = jnp.float32(0.0)
    for j in range(groups):
        count = count + jnp.where(tb_ref[0, j] == b, 1.0, 0.0)
    scale = 1.0 / jnp.maximum(jnp.full((1, 2 * raw.shape[1]), count, jnp.float32), 1.0)

    def gram(c):
        for e in range(bands):
            if e > 0:
                if c == 0:
                    own_copy(e).wait_recv()
                sum_copy(e, c).wait_recv()
            owner = lax.rem(b + bands - e, bands)
            for f in range(starts[c], starts[c] + sizes[c]):
                y = partner[owner, f]
                turned = jnp.concatenate([y[windows:], -y[:windows]], axis=0)
                both = jnp.concatenate([y, turned], axis=1)
                tile = lax.dot_general(
                    own[owner, f], both, (((0,), (0,)), ((), ())), preferred_element_type=jnp.float32
                )
                out_ref[owner * bins + f] = (tile * scale).astype(jnp.bfloat16)

    forward(0)
    for c in range(chunks):
        if c + 1 < chunks:
            forward(c + 1)
        band_sum(c)
        if c > 0:
            gram(c - 1)
    gram(chunks - 1)

    for e in range(1, bands):
        power_copy(e).wait_send()
        own_copy(e).wait_send()
    for t in range(len(others)):
        line_factor_copy(t).wait_send()
    for e in range(len(side)):
        side_factor_copy(e).wait_send()
    for c in range(chunks):
        for e in range(len(side)):
            first_copy(e, c).wait_send()
            for r in others:
                side_copy(e, r, c).wait_send()
        for e in range(1, bands):
            sum_copy(e, c).wait_send()
        for t in range(len(others)):
            own_line_copy(t, c).wait_send()


def local(groups, bands, spectra, tile_band):
    _, windows, bins, tile = spectra.shape
    rows = 2 * windows
    flat = spectra.reshape(rows * bins, tile)
    inner = groups // LINES
    dma = pltpu.SemaphoreType.DMA
    out = pl.pallas_call(
        functools.partial(kernel, groups, bands, bins, windows, CHUNKS),
        out_shape=jax.ShapeDtypeStruct((bands * bins, tile, 2 * tile), jnp.bfloat16),
        in_specs=[pl.BlockSpec(memory_space=pltpu.HBM)] * 2,
        out_specs=pl.BlockSpec(memory_space=pltpu.VMEM),
        scratch_shapes=[
            pltpu.SMEM((1, groups), jnp.int32),
            pltpu.VMEM((rows * bins, tile), jnp.bfloat16),
            pltpu.VMEM((rows * bins, tile), jnp.float32),
            pltpu.VMEM((bands, windows, tile), jnp.float32),
            pltpu.VMEM((LINES, bins, rows, tile), jnp.bfloat16),
            pltpu.VMEM((inner - 1, bins, rows, tile), jnp.bfloat16),
            pltpu.VMEM((LINES, windows, tile), jnp.float32),
            pltpu.VMEM((inner - 1, windows, tile), jnp.float32),
            pltpu.VMEM((groups, bins, rows, tile), jnp.bfloat16),
            pltpu.VMEM((bands - 1, bins, rows, tile), jnp.bfloat16),
            pltpu.VMEM((bands, bins, rows, tile), jnp.bfloat16),
            pltpu.VMEM((bands, bins, rows, tile), jnp.bfloat16),
            dma((2,)),
            dma((bands - 1,)),
            dma((bands - 1,)),
            dma((LINES - 1, CHUNKS)),
            dma((LINES, CHUNKS)),
            dma((inner - 1, CHUNKS)),
            dma((inner - 1, CHUNKS)),
            dma((inner - 1, LINES, CHUNKS)),
            dma((groups, CHUNKS)),
            dma((LINES - 1,)),
            dma((LINES,)),
            dma((inner - 1,)),
            dma((inner - 1,)),
            dma((bands - 1,)),
            dma((bands - 1,)),
            dma((bands - 1, CHUNKS)),
            dma((bands - 1, CHUNKS)),
        ],
        compiler_params=pltpu.CompilerParams(
            collective_id=0, has_side_effects=True, vmem_limit_bytes=32 * 1024 * 1024
        ),
    )(tile_band, flat)
    return out.reshape(1, 1, bands * bins, tile, 2 * tile)


def solution(mesh):
    return jax.shard_map(
        functools.partial(local, mesh.shape["grp"], mesh.shape["band"]),
        mesh=mesh,
        in_specs=(P(None, None, "band", "grp"), P("grp", None)),
        out_specs=P("grp", "band", None, None, None),
        check_vma=False,
    )
```

```python
import functools

import jax
import jax.numpy as jnp
from jax import lax
from jax.experimental import pallas as pl
from jax.experimental.pallas import tpu as pltpu
from jax.sharding import PartitionSpec as P

LINES = 4
SHARES = (1, 1, 1, 1)
CHUNKS = len(SHARES)
LEAD = 2
MESH = pl.DeviceIdType.MESH


def kernel(
    groups, bands, bins, windows, chunks,
    tb_hbm, x_hbm, out_ref,
    tb_ref, x_ref, raw, power, line_raw, side_raw, line_factor, side_factor, blocks, sums, own, partner,
    in_sem, p_send, p_recv, line_send, relay_send, line_recv, first_send, first_recv, side_send, block_recv,
    lf_send, lf_recv, sf_send, sf_recv, own_send, own_recv, sum_send, sum_recv,
):
    g = lax.axis_index("grp")
    b = lax.axis_index("band")
    inner = groups // LINES
    row, col = g // inner, lax.rem(g, inner)
    rows = 2 * windows
    unit = bins // sum(SHARES)
    sizes = [n * unit for n in SHARES]
    starts = [sum(sizes[:c]) for c in range(chunks)]
    half = row // 2
    others = [row + 1 - 2 * lax.rem(row, 2), 2 - half, 3 - 3 * half]
    side = [lax.rem(col + e, inner) for e in range(1, inner)]
    source = [lax.rem(col + inner - e, inner) for e in range(1, inner)]
    peer = [lax.rem(b + e, bands) for e in range(bands)]

    barrier = pltpu.get_barrier_semaphore()
    for r in others:
        pl.semaphore_signal(barrier, inc=1, device_id=(r * inner + col, b), device_id_type=MESH)
    for s in side:
        pl.semaphore_signal(barrier, inc=1, device_id=(row * inner + s, b), device_id_type=MESH)
    for k in peer[1:]:
        pl.semaphore_signal(barrier, inc=1, device_id=(g, k), device_id_type=MESH)

    load_x = pltpu.make_async_copy(x_hbm, x_ref, in_sem.at[0])
    load_tb = pltpu.make_async_copy(tb_hbm, tb_ref, in_sem.at[1])
    load_x.start()
    load_tb.start()
    load_x.wait()
    raw[...] = x_ref[...].astype(jnp.float32)
    total = jnp.zeros((rows, raw.shape[1]), jnp.float32)
    for f in range(bins):
        v = raw[pl.ds(f, rows, stride=bins), :]
        line_raw[row, f] = v.astype(jnp.bfloat16)
        total = total + v * v
    power[b] = total[:windows] + total[windows:]
    load_tb.wait()

    pl.semaphore_wait(barrier, len(others) + len(side) + bands - 1)

    def remote(src, dst, send_sem, recv_sem, target):
        return pltpu.make_async_remote_copy(
            src_ref=src, dst_ref=dst, send_sem=send_sem, recv_sem=recv_sem,
            device_id=target, device_id_type=MESH,
        )

    def power_copy(e):
        return remote(power.at[b], power.at[b], p_send.at[e - 1], p_recv.at[e - 1], (g, peer[e]))

    def line_copy(r, c, send_sem, to):
        view = line_raw.at[r, pl.ds(starts[c], sizes[c])]
        return remote(view, view, send_sem, line_recv.at[r, c], (to * inner + col, b))

    def own_line_copy(t, c):
        return line_copy(row, c, line_send.at[t, c], others[t])

    middle = (row > 0) & (row < LINES - 1)

    def relay_copy(c):
        return line_copy(others[-1], c, relay_send.at[c], (LINES - 1) * (row - 1))

    def send_line(c):
        own_line_copy(1, c).start()
        own_line_copy(0, c).start()

        @pl.when(middle)
        def _():
            own_line_copy(2, c).start()

    def first_copy(e, c):
        return remote(
            line_raw.at[row, pl.ds(starts[c], sizes[c])], side_raw.at[e, pl.ds(starts[c], sizes[c])],
            first_send.at[e, c], first_recv.at[e, c], (row * inner + side[e], b),
        )

    def side_copy(e, r, c):
        j = r * inner + col
        view = blocks.at[j, pl.ds(starts[c], sizes[c])]
        return remote(view, view, side_send.at[e, r, c], block_recv.at[j, c], (row * inner + side[e], b))

    def block_wait(j, c):
        view = blocks.at[j, pl.ds(starts[c], sizes[c])]
        remote(view, view, side_send.at[0, 0, c], block_recv.at[j, c], (g, peer[1])).wait_recv()

    def line_factor_copy(t):
        view = line_factor.at[row]
        return remote(view, view, lf_send.at[t], lf_recv.at[row], (others[t] * inner + col, b))

    def side_factor_copy(e):
        return remote(
            line_factor.at[row], side_factor.at[e], sf_send.at[e], sf_recv.at[e], (row * inner + side[e], b)
        )

    def own_copy(e):
        return remote(blocks.at[g], own.at[b], own_send.at[e - 1], own_recv.at[e - 1], (g, peer[e]))

    def sum_copy(e, c):
        span = pl.ds(starts[c], sizes[c])
        return remote(
            sums.at[e - 1, span], partner.at[b, span], sum_send.at[e - 1, c], sum_recv.at[e - 1, c], (g, peer[e])
        )

    def whiten(value, factor):
        both = jnp.concatenate([factor, factor], axis=0)
        return (value.astype(jnp.float32) * both).astype(jnp.bfloat16)

    for e in range(1, bands):
        power_copy(e).start()
    for c in range(chunks):
        for e in range(len(side)):
            first_copy(e, c).start()
        if c == 0:
            send_line(c)

    for e in range(1, bands):
        power_copy(e).wait_recv()
    whole = power[0]
    for e in range(1, bands):
        whole = whole + power[e]
    factor = lax.rsqrt(whole / (bins * bands) + 1e-05)
    line_factor[row] = factor
    for t in range(len(others)):
        line_factor_copy(t).start()
    for e in range(len(side)):
        side_factor_copy(e).start()
    for c in range(1, chunks):
        send_line(c)
    for f in range(bins):
        v = whiten(line_raw[row, f], factor)
        blocks[g, f] = v
        own[b, f] = v
    for e in range(1, bands):
        own_copy(e).start()
    def arrive(r, c):
        j = r * inner + col
        for f in range(starts[c], starts[c] + sizes[c]):
            blocks[j, f] = whiten(line_raw[r, f], line_factor[r])
        for e in range(len(side)):
            side_copy(e, r, c).start()

    def forward(c):
        for r in others:
            if c == 0:
                view = line_factor.at[r]
                remote(view, view, lf_send.at[0], lf_recv.at[r], (g, peer[1])).wait_recv()
            line_copy(r, c, line_send.at[0, c], others[0]).wait_recv()
            if r is others[-1]:
                @pl.when(middle)
                def _():
                    relay_copy(c).start()

            arrive(r, c)

    def pick(j, k):
        inside = (j >= 0) & (j < groups)
        at = jnp.clip(j, 0, groups - 1)
        return at, jnp.where(inside & (tb_ref[0, at] == k), 1.0, 0.0)

    reach = groups // bands

    def band_sum(c):
        for e in range(len(side)):
            if c == 0:
                side_factor_copy(e).wait_recv()
            first_copy(e, c).wait_recv()
            for f in range(starts[c], starts[c] + sizes[c]):
                blocks[row * inner + source[e], f] = whiten(side_raw[e, f], side_factor[e])
            for r in others:
                block_wait(r * inner + source[e], c)
        for e in list(range(1, bands)) + [0]:
            k = peer[e]
            terms = []
            for q in range(reach):
                d = k * reach + q
                terms.append(pick(g + d, k))
                at, weight = pick(g - d, k)
                terms.append((at, jnp.where(d > 0, weight, 0.0)))
            for f in range(starts[c], starts[c] + sizes[c]):
                acc = None
                for at, weight in terms:
                    term = blocks[at, f].astype(jnp.float32) * weight
                    acc = term if acc is None else acc + term
                acc = acc.astype(jnp.bfloat16)
                if e == 0:
                    partner[b, f] = acc
                else:
                    sums[e - 1, f] = acc
            if e > 0:
                sum_copy(e, c).start()

    count = jnp.float32(0.0)
    for j in range(groups):
        count = count + jnp.where(tb_ref[0, j] == b, 1.0, 0.0)
    scale = 1.0 / jnp.maximum(jnp.full((1, 2 * raw.shape[1]), count, jnp.float32), 1.0)

    def gram(c):
        for e in range(bands):
            if e > 0:
                if c == 0:
                    own_copy(e).wait_recv()
                sum_copy(e, c).wait_recv()
            owner = lax.rem(b + bands - e, bands)
            for f in range(starts[c], starts[c] + sizes[c]):
                y = partner[owner, f]
                turned = jnp.concatenate([y[windows:], -y[:windows]], axis=0)
                both = jnp.concatenate([y, turned], axis=1)
                tile = lax.dot_general(
                    own[owner, f], both, (((0,), (0,)), ((), ())), preferred_element_type=jnp.float32
                )
                out_ref[owner * bins + f] = (tile * scale).astype(jnp.bfloat16)

    for c in range(chunks + LEAD):
        if c < chunks:
            forward(c)
        if c >= LEAD:
            band_sum(c - LEAD)
        if c >= chunks:
            gram(c - chunks)
    for c in range(LEAD, chunks):
        gram(c)

    for e in range(1, bands):
        power_copy(e).wait_send()
        own_copy(e).wait_send()
    for t in range(len(others)):
        line_factor_copy(t).wait_send()
    for e in range(len(side)):
        side_factor_copy(e).wait_send()
    for c in range(chunks):
        for e in range(len(side)):
            first_copy(e, c).wait_send()
            for r in others:
                side_copy(e, r, c).wait_send()
        for e in range(1, bands):
            sum_copy(e, c).wait_send()
        for t in range(len(others) - 1):
            own_line_copy(t, c).wait_send()

        @pl.when(middle)
        def _():
            own_line_copy(2, c).wait_send()
            relay_copy(c).wait_send()


def local(groups, bands, spectra, tile_band):
    _, windows, bins, tile = spectra.shape
    rows = 2 * windows
    flat = spectra.reshape(rows * bins, tile)
    inner = groups // LINES
    dma = pltpu.SemaphoreType.DMA
    out = pl.pallas_call(
        functools.partial(kernel, groups, bands, bins, windows, CHUNKS),
        out_shape=jax.ShapeDtypeStruct((bands * bins, tile, 2 * tile), jnp.bfloat16),
        in_specs=[pl.BlockSpec(memory_space=pltpu.HBM)] * 2,
        out_specs=pl.BlockSpec(memory_space=pltpu.VMEM),
        scratch_shapes=[
            pltpu.SMEM((1, groups), jnp.int32),
            pltpu.VMEM((rows * bins, tile), jnp.bfloat16),
            pltpu.VMEM((rows * bins, tile), jnp.float32),
            pltpu.VMEM((bands, windows, tile), jnp.float32),
            pltpu.VMEM((LINES, bins, rows, tile), jnp.bfloat16),
            pltpu.VMEM((inner - 1, bins, rows, tile), jnp.bfloat16),
            pltpu.VMEM((LINES, windows, tile), jnp.float32),
            pltpu.VMEM((inner - 1, windows, tile), jnp.float32),
            pltpu.VMEM((groups, bins, rows, tile), jnp.bfloat16),
            pltpu.VMEM((bands - 1, bins, rows, tile), jnp.bfloat16),
            pltpu.VMEM((bands, bins, rows, tile), jnp.bfloat16),
            pltpu.VMEM((bands, bins, rows, tile), jnp.bfloat16),
            dma((2,)),
            dma((bands - 1,)),
            dma((bands - 1,)),
            dma((LINES - 1, CHUNKS)),
            dma((CHUNKS,)),
            dma((LINES, CHUNKS)),
            dma((inner - 1, CHUNKS)),
            dma((inner - 1, CHUNKS)),
            dma((inner - 1, LINES, CHUNKS)),
            dma((groups, CHUNKS)),
            dma((LINES - 1,)),
            dma((LINES,)),
            dma((inner - 1,)),
            dma((inner - 1,)),
            dma((bands - 1,)),
            dma((bands - 1,)),
            dma((bands - 1, CHUNKS)),
            dma((bands - 1, CHUNKS)),
        ],
        compiler_params=pltpu.CompilerParams(
            collective_id=0, has_side_effects=True, vmem_limit_bytes=32 * 1024 * 1024
        ),
    )(tile_band, flat)
    return out.reshape(1, 1, bands * bins, tile, 2 * tile)


def solution(mesh):
    return jax.shard_map(
        functools.partial(local, mesh.shape["grp"], mesh.shape["band"]),
        mesh=mesh,
        in_specs=(P(None, None, "band", "grp"), P("grp", None)),
        out_specs=P("grp", "band", None, None, None),
        check_vma=False,
    )
```
